32 devices in a mesh: expert: 4 (over y, core), tensor: 4 (over z), dp: 2 (over x).
Axes of the slice: x: 2, y: 2, z: 4, core: 2. Of those that a mesh axis runs over, the one named last changes fastest.
Arguments:
- tokens: bfloat16 [1024, 3072], P(('expert', 'dp')), may hold values from -6 to 6
- chosen_logits: float32 [1024, 2], P(('expert', 'dp')), may hold values from -6 to 6
- routes: int32 [1024, 2], replicated, may hold values from 0 to 3, all different within a row; in each aligned block of 128 rows (0 to 127, 128 to 255, ...) at most 80 rows name the same one
- forget_flag: int32 [1024], replicated, may hold values 0 or 1
- steer: float32 [3072], replicated, may hold values from -6 to 6
- w_gate: bfloat16 [4, 3072, 8192], P('expert', 'dp', 'tensor'), may hold values from -0.109375 to 0.109375
- w_up: bfloat16 [4, 3072, 8192], P('expert', 'dp', 'tensor'), may hold values from -0.109375 to 0.109375
- down_frozen: bfloat16 [4, 3072, 8192], P('expert', 'dp', 'tensor'), may hold values from -0.0625 to 0.0625
- down_trained: bfloat16 [4, 3072, 8192], P('expert', 'dp', 'tensor'), may hold values from -0.0625 to 0.0625
Outputs:
- grad_down: bfloat16 [4, 3072, 8192], P('expert', 'dp', 'tensor')
The draws below stay inside these ranges and needn't reach their ends.
Inputs may be any that keep to these rules, and one draw needn't show every extreme that they name: `routes`: the two experts of a row differ. In each aligned block of 128 rows (the tokens of one index of expert and dp, blocks ordered by expert index, then dp index) no expert is named by more than 80 rows, and one expert is named by exactly 80 rows in some block of every draw.
All inputs are finite; a program needn't handle non-finite values.
Results may differ from the reference program's by a relative error of at most 0.0063.
Values may be sent and summed in bfloat16 or wider, within the bound.
No kernel may reach another device: no remote copies, remote signals or barrier semaphores. Data moves between devices by JAX's collectives and lax.ppermute only.
A program may use at most 192 MiB of HBM per device.

```python
import math
import jax
import jax.numpy as jnp
import numpy as np
from jax import lax

D = 3072
FF = 8192
TOP = 2
TOK_DEV = 128
EXPERTS = 4
CAP = 80
TOKENS = 1024
N_EXPERT = 4
N_DP = 2


def place_ends(array, key, least, top_value):
    place = [jax.random.randint(jax.random.fold_in(key, axis), (), 0, length) for axis, length in enumerate(array.shape)]
    widest = array.shape.index(max(array.shape))
    beside = place[:widest] + [(place[widest] + 1) % array.shape[widest]] + place[widest + 1:]
    return array.at[tuple(place)].set(least).at[tuple(beside)].set(top_value)


def steps_of(rng, dims, shards, smallest, high):
    level = 1.0
    for axis_at, parts in shards:
        heights = jax.random.uniform(jax.random.fold_in(jax.random.fold_in(rng, 6), axis_at), (parts,), jnp.float32, smallest / len(shards), high / len(shards))
        level = level * jnp.repeat(jnp.exp(heights), dims[axis_at] // parts).reshape((-1,) + (1,) * (len(dims) - 1 - axis_at))
    return level


def shared_out(stream_key, own, number, rows, amount, top, bound, lean):
    ranking = jax.random.permutation(stream_key, amount)
    crowded, common = load_shares(amount, rows * top, bound, lean, True), load_shares(amount, rows * top, bound, lean, False)
    places = jnp.arange(amount)

    def named(sizes, rotation):
        used = int((sizes > 0).sum())
        fixed = max(1, used // 4)
        moved = fixed + (places - fixed + rotation * (used - fixed)) % max(1, amount - fixed)
        return jnp.zeros((amount,), jnp.int32).at[ranking[jnp.where(places < fixed, places, moved)]].set(jnp.asarray(sizes, jnp.int32))

    sizes = jnp.where(number % 4 == 0, named(crowded, number // 4), named(common, number - number // 4 - 1))
    mixed = jax.random.permutation(jax.random.fold_in(own, 3), amount)
    giver, receiver = mixed[0:amount // 2 * 2:2], mixed[1:amount // 2 * 2:2]
    room = jnp.minimum(sizes[giver] - 1, bound - sizes[receiver]) // 2
    room = jnp.where((giver == ranking[0]) | (receiver == ranking[0]) | (sizes[receiver] == 0), 0, jnp.maximum(room, 0))
    moved = jax.random.randint(jax.random.fold_in(own, 4), (amount // 2,), 0, 1 << 20) % (room + 1)
    sizes = sizes.at[giver].add(-moved).at[receiver].add(moved)
    labels = jnp.searchsorted(jnp.cumsum(sizes), jnp.arange(rows * top), side="right").astype(jnp.int32)
    grid = labels.reshape(top, rows).T
    grid = grid[jax.random.permutation(jax.random.fold_in(own, 1), rows)]
    rotation = jax.random.randint(jax.random.fold_in(own, 2), (rows, 1), 0, top)
    return jnp.take_along_axis(grid, (jnp.arange(top)[None, :] + rotation) % top, axis=1)


def load_shares(number_of, total, limit, slope, full):
    portions = [(1 << 20) // math.isqrt(grade ** slope) + 1 for grade in range(1, number_of + 1)]
    largest = limit if full else min(limit, max(-(-total // number_of), total * portions[0] // sum(portions)))
    least = 1 if total - largest >= number_of - 1 else 0
    counts, spare = [largest] + [least] * (number_of - 1), total - largest - least * (number_of - 1)
    while spare > 0:
        candidates = [i for i in range(1, number_of) if counts[i] < largest] or [i for i in range(1, number_of) if counts[i] < limit]
        whole, budget = sum([portions[i] for i in candidates]), spare
        for i in candidates:
            more = min(limit - counts[i], max(1, budget * portions[i] // whole), spare)
            counts[i] = counts[i] + more
            spare = spare - more
    return np.array(counts)


def centred(own_key, extent, spread, reach, pieces=(), kind=jnp.bfloat16):
    gain = steps_of(own_key, extent, pieces, -0.22, 0.18) if pieces else 1.0
    result = jax.random.normal(own_key, extent, jnp.float32) * spread * gain
    return jnp.minimum(jnp.maximum(result, -reach), reach).astype(kind)


def setup_inputs(seed: int = 0) -> dict:
    arg_keys = jax.random.split(jax.random.key(seed), 10)
    tokens = centred(arg_keys[0], (TOKENS, D), 1.0, 6.0, ((0, 8),))
    chosen_logits = centred(arg_keys[1], (TOKENS, TOP), 1.5, 6.0, ((0, 8),), jnp.float32)
    routes_keys = jax.random.split(jax.random.fold_in(arg_keys[2], 1), TOKENS // TOK_DEV)
    routes_turns = jax.random.permutation(jax.random.fold_in(arg_keys[2], 3), TOKENS // TOK_DEV)
    routes = jax.vmap(lambda own, number: shared_out(jax.random.fold_in(arg_keys[2], 2), own, number, TOK_DEV, EXPERTS, TOP, CAP, 2))(routes_keys, routes_turns).reshape((TOKENS, TOP))
    forget_flag = place_ends((jax.random.randint(arg_keys[3], (TOKENS,), 0, 2) < 1).astype(jnp.int32), jax.random.fold_in(arg_keys[3], 1), 0, 1)
    steer = centred(arg_keys[4], (D,), 1.0, 6.0, (), jnp.float32)
    w_gate = centred(arg_keys[5], (EXPERTS, D, FF), D ** -0.5, 0.109375, ((0, 4), (1, 2), (2, 4)))
    w_up = centred(arg_keys[6], (EXPERTS, D, FF), D ** -0.5, 0.109375, ((0, 4), (1, 2), (2, 4)))
    down_frozen = centred(arg_keys[7], (EXPERTS, D, FF), FF ** -0.5, 0.0625, ((0, 4), (1, 2), (2, 4)))
    down_trained = centred(arg_keys[8], (EXPERTS, D, FF), FF ** -0.5, 0.0625, ((0, 4), (1, 2), (2, 4)))
    return dict(tokens=tokens, chosen_logits=chosen_logits, routes=routes, forget_flag=forget_flag, steer=steer, w_gate=w_gate, w_up=w_up, down_frozen=down_frozen, down_trained=down_trained)


forget_coef = 0.0625
retain_coef = 0.125


def reference(tokens, chosen_logits, routes, forget_flag, steer, w_gate, w_up, down_frozen, down_trained):
    first_w = 1.0 / (1.0 + jnp.exp(chosen_logits[:, 1] - chosen_logits[:, 0]))
    route_w = jnp.stack([first_w, 1.0 - first_w], axis=1)
    forget = forget_flag.astype(jnp.float32)
    retain = 1.0 - forget
    pair_count = 2 * TOKENS
    pair_expert = routes.reshape(-1).astype(jnp.int32)
    pair_index = jnp.arange(pair_count, dtype=jnp.int32)
    pair_token = pair_index // 2
    pair_weight = route_w.reshape(-1)
    load_rows = N_EXPERT * N_DP * CAP

    def forward(packed):
        expert_id, gate_mat, up_mat, frozen_mat, trained_mat = packed
        sort_key = jnp.where(pair_expert == expert_id, 0, 1).astype(jnp.int32) * pair_count + pair_index
        sort_order = jnp.argsort(sort_key)[:load_rows]
        is_valid = (pair_expert[sort_order] == expert_id).astype(jnp.float32)
        token_ids = pair_token[sort_order]
        token_rows = tokens[token_ids]
        gate_pre = jnp.dot(token_rows, gate_mat, preferred_element_type=jnp.float32)
        up_pre = jnp.dot(token_rows, up_mat, preferred_element_type=jnp.float32)
        hidden = (jax.nn.silu(gate_pre) * up_pre).astype(jnp.bfloat16)
        trained_out = jnp.dot(hidden, trained_mat.T, preferred_element_type=jnp.float32)
        frozen_out = jnp.dot(hidden, frozen_mat.T, preferred_element_type=jnp.float32)
        change = trained_out - retain[token_ids][:, None] * frozen_out
        return hidden, change, token_ids, is_valid * pair_weight[sort_order]

    expert_iota = jnp.arange(EXPERTS, dtype=jnp.int32)
    hiddens, changes, token_ids, weights = lax.map(forward, (expert_iota, w_gate, w_up, down_frozen, down_trained))
    combined = jnp.zeros((TOKENS, D), jnp.float32).at[token_ids.reshape(-1)].add(
        weights.reshape(-1, 1) * changes.reshape(-1, D))
    residual = combined + forget[:, None] * (tokens.astype(jnp.float32) - steer[None, :])
    token_err = residual * (retain_coef - (retain_coef - forget_coef) * forget)[:, None]

    def backward(packed):
        hidden, ids, weight = packed
        slot_err = (weight[:, None] * token_err[ids]).astype(jnp.bfloat16)
        return jnp.dot(slot_err.T, hidden, preferred_element_type=jnp.float32).astype(jnp.bfloat16)

    return lax.map(backward, (hiddens, token_ids, weights))
```

```python
import jax
import jax.numpy as jnp
from jax import lax
from jax.sharding import PartitionSpec as P

TOP = 2
BF16 = jnp.bfloat16
F32 = jnp.float32

forget_coef = 0.0625
retain_coef = 0.125


def xor_permute(block, axis, mask):
    size = lax.axis_size(axis)
    return lax.ppermute(block, axis, [(i, i ^ mask) for i in range(size)])


def bits_of(size):
    return [1 << b for b in range(size.bit_length() - 1)]


def reversed_order(size):
    order = [0]
    for bit in bits_of(size)[::-1]:
        order = order + [j | bit for j in order]
    return order


def gather_blocks(block, axis):
    size = lax.axis_size(axis)
    blocks = {0: block}
    for bit in bits_of(size)[::-1]:
        for j in list(blocks):
            blocks[j ^ bit] = xor_permute(blocks[j], axis, bit)
    return [blocks[j] for j in range(size)]


def scatter_sum(rows, axis):
    for bit in bits_of(lax.axis_size(axis)):
        half = rows.shape[0] // 2
        came = xor_permute(rows[half:].astype(BF16), axis, bit)
        rows = rows[:half] + came.astype(F32)
    return rows


def scatter_sum_direct(rows, axis):
    size = lax.axis_size(axis)
    part = rows.shape[0] // size
    total = rows[:part]
    for j in range(1, size):
        came = xor_permute(rows[j * part:(j + 1) * part].astype(BF16), axis, j)
        total = total + came.astype(F32)
    return total


def slot_table(group_routes, expert, capacity):
    member = jnp.any(group_routes == expert, axis=2).astype(jnp.int32)
    position = jnp.cumsum(member, axis=1) - member
    return jnp.where(member > 0, position, -1)


def local(
    tokens, chosen_logits, routes, forget_flag, steer, w_gate, w_up, down_frozen, down_trained
):
    n_exp = lax.axis_size("expert")
    n_ten = lax.axis_size("tensor")
    n_dp = lax.axis_size("dp")
    n_tok = tokens.shape[0]
    width = w_gate.shape[1]
    cap = min(n_tok, n_tok * TOP // n_exp + n_tok * TOP // (4 * n_exp))
    me = lax.axis_index("expert")
    my_ten = lax.axis_index("tensor")
    my_dp = lax.axis_index("dp")
    w_gate, w_up, down_frozen, down_trained = w_gate[0], w_up[0], down_frozen[0], down_trained[0]
    n_chunk = max(1, min(n_exp, n_tok * n_dp // n_ten // 16))
    per_chunk = n_exp // n_chunk

    mine = lax.dynamic_slice_in_dim(tokens, my_dp * width, width, 1)
    other = lax.dynamic_slice_in_dim(tokens, (1 - my_dp) * width, width, 1)
    near = jnp.concatenate(gather_blocks(mine, "expert"), axis=0)
    far = jnp.concatenate(gather_blocks(xor_permute(other, "dp", 1), "expert"), axis=0)
    first_w = 1.0 / (1.0 + jnp.exp(chosen_logits[:, 1] - chosen_logits[:, 0]))
    all_w = lax.all_gather(first_w, ("expert", "dp"), axis=0, tiled=True)
    all_w = all_w.reshape(n_exp, n_dp, n_tok)
    all_routes = routes.reshape(n_exp, n_dp, n_tok, TOP)
    all_flags = forget_flag.reshape(n_exp, n_dp, n_tok).astype(F32)
    relative = me ^ jnp.arange(n_exp, dtype=jnp.int32)

    def side(dp):
        pick = lambda a: lax.dynamic_index_in_dim(a, dp, 1, keepdims=False)
        group_routes, weight, flag = pick(all_routes), pick(all_w), pick(all_flags)
        slot = slot_table(group_routes, me, cap)
        weight = jnp.where(group_routes[:, :, 0] == me, weight, 1.0 - weight)
        return slot, weight, flag

    slot_iota = jnp.arange(cap, dtype=jnp.int32)
    sides = [side(my_dp), side(1 - my_dp)]

    def slot_rows(slot, tokens_of):
        table = jnp.where(slot < 0, -1, slot + jnp.arange(n_exp, dtype=jnp.int32)[:, None] * cap)
        table = jnp.take(table, relative, axis=0).reshape(-1)
        hit = jnp.arange(n_exp * cap, dtype=jnp.int32)[:, None] == table[None, :]
        return jnp.dot(hit.astype(BF16), tokens_of, preferred_element_type=F32).astype(BF16)

    def of_slots(slot, value):
        hit = slot_iota[None, :, None] == slot[:, None, :]
        return jnp.sum(jnp.where(hit, value[:, None, :], 0.0), axis=2)

    near_rows = slot_rows(sides[0][0], near)
    far_rows = slot_rows(sides[1][0], far)
    scale = [of_slots(s, w).reshape(-1, 1) for s, w, _ in sides]
    retain = [of_slots(s, 1.0 - f).reshape(-1, 1) for s, _, f in sides]

    chunk_slots = per_chunk * cap
    chunk_tok = per_chunk * n_tok
    hiddens, sums, orders = [], [], []
    order = jnp.asarray(reversed_order(n_exp), jnp.int32)
    tok_order_e = me ^ order
    tok_order_t = my_ten ^ jnp.arange(n_ten, dtype=jnp.int32)
    share = chunk_tok // (n_exp * n_ten)

    def ordered(value):
        v = value.reshape(n_exp, n_ten, share)
        return jnp.take(jnp.take(v, tok_order_e, axis=0), tok_order_t, axis=1)

    for c in range(n_chunk):
        rows = slice(c * chunk_slots, (c + 1) * chunk_slots)
        groups = slice(c * per_chunk, (c + 1) * per_chunk)
        came_gate = xor_permute(
            jnp.dot(near_rows[rows], w_gate, preferred_element_type=F32).astype(BF16), "dp", 1)
        came_up = xor_permute(
            jnp.dot(near_rows[rows], w_up, preferred_element_type=F32).astype(BF16), "dp", 1)
        gate = jnp.dot(far_rows[rows], w_gate, preferred_element_type=F32) + came_gate.astype(F32)
        up = jnp.dot(far_rows[rows], w_up, preferred_element_type=F32) + came_up.astype(F32)
        far_hidden = (jax.nn.silu(gate) * up).astype(BF16)
        near_hidden = xor_permute(far_hidden, "dp", 1)
        hidden = jnp.concatenate([near_hidden, far_hidden], axis=0)
        contract = (((1,), (1,)), ((), ()))
        trained = lax.dot_general(hidden, down_trained, contract, preferred_element_type=F32)
        frozen = lax.dot_general(hidden, down_frozen, contract, preferred_element_type=F32)
        keep = jnp.concatenate([retain[0][rows], retain[1][rows]], axis=0)
        weight = jnp.concatenate([scale[0][rows], scale[1][rows]], axis=0)
        change = (weight * (trained - keep * frozen)).astype(BF16)
        tables = []
        for k in range(2):
            slot = sides[k][0][groups]
            base = k * chunk_slots + jnp.arange(per_chunk, dtype=jnp.int32)[:, None] * cap
            tables.append(ordered(jnp.where(slot < 0, -1, slot + base)))
        table = jnp.stack(tables, axis=2).reshape(-1)
        put = (table[:, None] == jnp.arange(2 * chunk_slots, dtype=jnp.int32)[None, :]).astype(BF16)
        part = jnp.dot(put, change, preferred_element_type=F32)
        summed = scatter_sum_direct(scatter_sum(part, "expert"), "tensor")
        hiddens.append(hidden)
        sums.append((summed, put, weight))

    near3 = near.reshape(n_exp, n_tok, width)
    far3 = far.reshape(n_exp, n_tok, width)
    slot_errs = []
    for c in range(n_chunk):
        summed, put, weight = sums[c]
        groups = slice(c * per_chunk, (c + 1) * per_chunk)
        first = (me * n_ten + my_ten) * share
        own_tok, own_flag = [], []
        for k, blocks in enumerate((near3, far3)):
            group = c * per_chunk + first // n_tok
            at = first % n_tok
            own_tok.append(lax.dynamic_slice(
                blocks, (me ^ group, at, 0), (1, share, width))[0])
            own_flag.append(lax.dynamic_slice(sides[k][2], (group, at), (1, share))[0])
        own_tok = jnp.concatenate(own_tok, axis=0).astype(F32)
        flag = jnp.concatenate(own_flag, axis=0)[:, None]
        my_steer = lax.dynamic_slice_in_dim(steer, my_dp * width, width, 0)
        residual = summed + flag * (own_tok - my_steer[None, :])
        err = (residual * (retain_coef - (retain_coef - forget_coef) * flag)).astype(BF16)
        err = jnp.concatenate(
            [err] + [xor_permute(err, "tensor", j) for j in range(1, n_ten)], axis=0)
        for bit in bits_of(n_exp)[::-1]:
            err = jnp.concatenate([err, xor_permute(err, "expert", bit)], axis=0)
        picked = lax.dot_general(put, err, (((0,), (0,)), ((), ())), preferred_element_type=F32)
        slot_errs.append((weight * picked).astype(BF16))
    grad = lax.dot_general(
        jnp.concatenate(slot_errs, axis=0), jnp.concatenate(hiddens, axis=0),
        (((0,), (0,)), ((), ())), preferred_element_type=F32)
    return grad.astype(BF16)[None]


def solution(mesh):
    in_specs = (
        P(("expert", "dp"), None),
        P(("expert", "dp"), None),
        P(),
        P(),
        P(),
        P("expert", "dp", "tensor"),
        P("expert", "dp", "tensor"),
        P("expert", "dp", "tensor"),
        P("expert", "dp", "tensor"),
    )
    out_specs = P("expert", "dp", "tensor")
    return jax.shard_map(local, mesh=mesh, in_specs=in_specs, out_specs=out_specs, check_vma=False)
```

```python
import jax
import jax.numpy as jnp
from jax import lax
from jax.experimental import pallas as pl
from jax.experimental.pallas import tpu as pltpu
from jax.sharding import PartitionSpec as P

TOP = 2
BF16 = jnp.bfloat16
F32 = jnp.float32

forget_coef = 0.0625
retain_coef = 0.125


def xor_permute(block, axis, mask):
    size = lax.axis_size(axis)
    return lax.ppermute(block, axis, [(i, i ^ mask) for i in range(size)])


def bits_of(size):
    return [1 << b for b in range(size.bit_length() - 1)]


def reversed_order(size):
    order = [0]
    for bit in bits_of(size)[::-1]:
        order = order + [j | bit for j in order]
    return order


def gather_blocks(block, axis):
    size = lax.axis_size(axis)
    blocks = {0: block}
    for bit in bits_of(size)[::-1]:
        for j in list(blocks):
            blocks[j ^ bit] = xor_permute(blocks[j], axis, bit)
    return [blocks[j] for j in range(size)]


class Order:
    def __init__(self):
        self.last = None

    def after(self, value, *others):
        others = others + (() if self.last is None else (self.last,))
        return lax.optimization_barrier((value, others))[0] if others else value

    def done(self, value):
        self.last = value
        return value


LITTLE = pl.CostEstimate(flops=0, bytes_accessed=0, transcendentals=0)


def params(mib):
    return pltpu.CompilerParams(vmem_limit_bytes=mib * 1024 * 1024)


def vmem():
    return pl.BlockSpec(memory_space=pltpu.VMEM)


def project_kernel(n_blocks, bounds, table_ref, *refs):
    blocks, weights = refs[:n_blocks], refs[n_blocks:n_blocks + 2]
    outs, (tok_ref, row_ref) = refs[n_blocks + 2:-2], refs[-2:]
    size = blocks[0].shape[0]
    for j in range(n_blocks):
        tok_ref[j * size:(j + 1) * size] = blocks[j][...]
    slot = lax.broadcasted_iota(jnp.int32, (row_ref.shape[0], n_blocks * size), 0)
    hit = (table_ref[...] == slot).astype(F32).astype(BF16)
    row_ref[...] = jnp.dot(hit, tok_ref[...], preferred_element_type=F32).astype(BF16)
    ff = weights[0].shape[1]
    tile = min(ff, 512)
    for at, weight in enumerate(weights):
        for left in range(0, ff, tile):
            product = jnp.dot(row_ref[...], weight[:, left:left + tile], preferred_element_type=F32)
            for out, (first, last) in zip(outs, bounds):
                out[at, :, left:left + tile] = product[first:last].astype(out.dtype)


def project(table, blocks, w_gate, w_up, bounds, dtype):
    depth, ff = w_gate.shape
    n_blocks = len(blocks)
    size = blocks[0].shape[0]
    return pl.pallas_call(
        lambda *refs: project_kernel(n_blocks, bounds, *refs),
        in_specs=[vmem()] * (n_blocks + 3),
        out_specs=[vmem()] * len(bounds),
        out_shape=[jax.ShapeDtypeStruct((2, b - a, ff), dtype) for a, b in bounds],
        scratch_shapes=[pltpu.VMEM((n_blocks * size, depth), BF16),
                        pltpu.VMEM((bounds[-1][1], depth), BF16)],
        compiler_params=params(12),
        cost_estimate=LITTLE,
    )(table, *blocks, w_gate, w_up)


def hide_kernel(kept_ref, came_ref, out_ref):
    gate = kept_ref[0] + came_ref[0].astype(F32)
    up = kept_ref[1] + came_ref[1].astype(F32)
    out_ref[...] = (gate / (1.0 + jnp.exp(-gate)) * up).astype(BF16)


def hide(kept, came):
    _, rows, ff = kept.shape
    return pl.pallas_call(
        hide_kernel,
        in_specs=[vmem()] * 2,
        out_specs=vmem(),
        out_shape=jax.ShapeDtypeStruct((rows, ff), BF16),
        compiler_params=params(12),
        cost_estimate=LITTLE,
    )(kept, came)


def down_kernel(near_ref, far_ref, trained_ref, frozen_ref, coef_ref, table_ref, keep_ref, send_ref, hid_ref):
    slots = near_ref.shape[0]
    hid_ref[:slots] = near_ref[...]
    hid_ref[slots:] = far_ref[...]
    contract = (((1,), (1,)), ((), ()))
    slot = lax.broadcasted_iota(jnp.int32, (table_ref.shape[0], 2 * slots), 1)
    put = (table_ref[...] == slot).astype(F32).astype(BF16)
    half = put.shape[0] // 2
    width = trained_ref.shape[0]
    tile = 256
    for left in range(0, width, tile):
        cols = slice(left, left + tile)
        hidden = hid_ref[...]
        trained = lax.dot_general(hidden, trained_ref[cols], contract, preferred_element_type=F32)
        frozen = lax.dot_general(hidden, frozen_ref[cols], contract, preferred_element_type=F32)
        change = coef_ref[:, 0:1] * trained - coef_ref[:, 1:2] * frozen
        high = change.astype(BF16)
        low = (change - high.astype(F32)).astype(BF16)
        part = (jnp.dot(put, high, preferred_element_type=F32)
                + jnp.dot(put, low, preferred_element_type=F32))
        keep_ref[:, cols] = part[:half]
        send_ref[:, cols] = part[half:].astype(BF16)


def down(near, far, trained, frozen, coef, table):
    slots, ff = near.shape
    width = trained.shape[0]
    rows = table.shape[0]
    return pl.pallas_call(
        down_kernel,
        in_specs=[vmem()] * 6,
        out_specs=[vmem()] * 2,
        out_shape=[
            jax.ShapeDtypeStruct((rows // 2, width), F32),
            jax.ShapeDtypeStruct((rows // 2, width), BF16),
        ],
        scratch_shapes=[pltpu.VMEM((2 * slots, ff), BF16)],
        compiler_params=params(12),
        cost_estimate=LITTLE,
    )(near, far, trained, frozen, coef, table)


def slot_table(group_routes, expert, capacity):
    member = jnp.any(group_routes == expert, axis=2).astype(jnp.int32)
    position = jnp.cumsum(member, axis=1) - member
    return jnp.where(member > 0, position, -1)


def local(
    tokens, chosen_logits, routes, forget_flag, steer, w_gate, w_up, down_frozen, down_trained
):
    n_exp = lax.axis_size("expert")
    n_ten = lax.axis_size("tensor")
    n_dp = lax.axis_size("dp")
    n_tok = tokens.shape[0]
    width = w_gate.shape[1]
    cap = min(n_tok, n_tok * TOP // n_exp + n_tok * TOP // (4 * n_exp))
    me = lax.axis_index("expert")
    my_dp = lax.axis_index("dp")
    w_gate, w_up, down_frozen, down_trained = w_gate[0], w_up[0], down_frozen[0], down_trained[0]
    if n_tok * n_dp // n_ten >= 64:
        sizes = [n_exp // 4] * 4
    else:
        sizes = [n_exp]
    n_chunk = len(sizes)
    starts = [sum(sizes[:c]) for c in range(n_chunk)]

    order = Order()
    all_routes = routes.reshape(n_exp, n_dp, n_tok, TOP)
    all_flags = forget_flag.reshape(n_exp, n_dp, n_tok).astype(F32)
    relative = me ^ jnp.arange(n_exp, dtype=jnp.int32)
    exp_order = jnp.asarray(reversed_order(n_exp), jnp.int32)
    shares = [size * n_tok // n_exp for size in sizes]

    first_w = 1.0 / (1.0 + jnp.exp(chosen_logits[:, 1] - chosen_logits[:, 0]))
    other_w = xor_permute(first_w, "dp", 1)
    mine = lax.dynamic_slice_in_dim(tokens, my_dp * width, width, 1)
    other = lax.dynamic_slice_in_dim(tokens, (1 - my_dp) * width, width, 1)
    near = gather_blocks(mine, "expert")
    far = gather_blocks(xor_permute(other, "dp", 1), "expert")

    def side(a, dp):
        return lax.dynamic_index_in_dim(a, dp, 1, keepdims=False)

    side_routes = [side(all_routes, my_dp), side(all_routes, 1 - my_dp)]
    side_flags = [side(all_flags, my_dp), side(all_flags, 1 - my_dp)]
    slots = [slot_table(r, me, cap) for r in side_routes]
    slot_iota = jnp.arange(cap, dtype=jnp.int32)

    def row_table(slot):
        table = jnp.where(slot < 0, -1, slot + jnp.arange(n_exp, dtype=jnp.int32)[:, None] * cap)
        return jnp.take(table, relative, axis=0).reshape(1, -1)

    def swap(value):
        return xor_permute(value, "dp", 1)

    def groups_of(c):
        return slice(starts[c], starts[c] + sizes[c])

    bounds = [(starts[c] * cap, (starts[c] + sizes[c]) * cap) for c in range(n_chunk)]
    sent = order.done(project(row_table(slots[0]), near, w_gate, w_up, bounds, BF16))
    came = [swap(v) for v in sent[:2]] + [None] * (n_chunk - 2)
    own_w = order.after(jnp.stack([first_w, other_w], axis=0))
    w_blocks = gather_blocks(own_w, "expert")
    far_table, *far_blocks = order.after([row_table(slots[1])] + far)
    kept = order.done(project(far_table, far_blocks, w_gate, w_up, bounds, F32))

    def make_tables():
        all_w = jnp.take(jnp.stack(w_blocks, axis=0), relative, axis=0)
        late_slots, late_near, late_far = order.after((jnp.stack(slots, axis=0), near, far))
        late_flags = jnp.stack(side_flags, axis=0)
        late_routes = jnp.stack(side_routes, axis=0)
        weight = jnp.where(late_routes[:, :, :, 0] == me, all_w.swapaxes(0, 1), 1.0 - all_w.swapaxes(0, 1))
        in_slot = slot_iota[None, None, :, None] == late_slots[:, :, None, :]
        spread_w = jnp.where(in_slot, weight[:, :, None, :], 0.0)
        scale = jnp.sum(spread_w, axis=3)
        coefs = jnp.stack([scale, jnp.sum(spread_w * (1.0 - late_flags)[:, :, None, :], axis=3)], axis=3)
        tables, biases, factors = [], [], []
        my_steer = lax.dynamic_slice_in_dim(steer, my_dp * width, width, 0)
        tok_blocks = (jnp.stack(late_near, axis=0), jnp.stack(late_far, axis=0))
        is_taker = (exp_order ^ me)[:, None] == jnp.arange(n_exp, dtype=jnp.int32)[None, :]
        for c in range(n_chunk):
            share = shares[c]
            slot = late_slots[:, groups_of(c)]
            base = (jnp.arange(2, dtype=jnp.int32)[:, None, None] * (sizes[c] * cap)
                    + jnp.arange(sizes[c], dtype=jnp.int32)[None, :, None] * cap)
            table = jnp.where(slot < 0, -1, slot + base).reshape(2, n_exp, share).swapaxes(0, 1)
            table = jnp.sum(jnp.where(is_taker[:, :, None, None], table[None], 0), axis=1)
            tables.append(table.reshape(-1, 1))
            first = me * share
            group, at = starts[c] + first // n_tok, first % n_tok
            own_tok = jnp.concatenate([
                lax.dynamic_slice(b, (me ^ group, at, 0), (1, share, width))[0] for b in tok_blocks], axis=0)
            flag = lax.dynamic_slice(late_flags, (0, group, at), (2, 1, share)).reshape(-1, 1)
            biases.append(flag * (own_tok.astype(F32) - my_steer[None, :]))
            factors.append(retain_coef - (retain_coef - forget_coef) * flag)
        return order.done(lax.optimization_barrier((scale, coefs, tables, biases, factors)))

    far_hidden, near_hidden = [None] * n_chunk, [None] * n_chunk

    def make_hidden(c):
        far_hidden[c] = order.done(hide(order.after(kept[c]), came[c]))
        near_hidden[c] = swap(far_hidden[c])

    def send_sums(c):
        came[c] = swap(order.after(sent[c]))

    exp_bits, ten_bits = bits_of(n_exp), bits_of(n_ten)[::-1]
    sums = [None] * n_chunk
    to_send = [None] * n_chunk
    spread = [None] * n_chunk

    def change(c):
        coef = jnp.concatenate(
            [coefs[k][groups_of(c)].reshape(-1, 2) for k in range(2)], axis=0)
        keep, send = order.done(down(
            order.after(near_hidden[c]), far_hidden[c], down_trained, down_frozen, coef, tables[c]))
        sums[c] = (keep, xor_permute(send, "expert", 1))

    def add(c, bit):
        keep, got = sums[c]
        total = order.after(keep) + got.astype(F32)
        if 2 * bit < n_exp:
            half = total.shape[0] // 2
            keep, send = order.done((total[:half], total[half:].astype(BF16)))
            sums[c] = (keep, xor_permute(send, "expert", 2 * bit))
            return
        spread_over(c, order.done(total), 0)

    def spread_over(c, total, step):
        bit = ten_bits[step]
        sums[c] = (total, xor_permute(total.astype(BF16), "tensor", bit))

    def add_tensor(c, step):
        keep, got = sums[c]
        total = order.after(keep) + got.astype(F32)
        if step + 1 < len(ten_bits):
            spread_over(c, order.done(total), step + 1)
            return
        spread[c] = order.done(((total + biases[c]) * factors[c]).astype(BF16))
        widen(c, exp_bits[-1])

    def widen(c, bit):
        got = xor_permute(spread[c], "expert", bit)
        spread[c] = [spread[c], got]

    def join(c, bit):
        err = order.done(jnp.concatenate(order.after(spread[c]), axis=0))
        spread[c] = err
        if bit:
            widen(c, bit)


    def add_high(c):
        for bit in exp_bits[1:]:
            add(c, bit)

    def add_tensor_rest(c):
        for step in range(1, len(ten_bits)):
            add_tensor(c, step)

    def join_rest(c):
        for bit in exp_bits[::-1][1:]:
            join(c, bit)

    low = exp_bits[0]
    make_hidden(0)
    scale, coefs, tables, biases, factors = make_tables()
    if n_chunk == 1:
        change(0)
        add(0, low)
        add_high(0)
        add_tensor(0, 0)
        add_tensor_rest(0)
        join_rest(0)
    else:
        send_sums(2)
        make_hidden(1)
        change(0)
        add(0, low)
        send_sums(3)
        make_hidden(2)
        add_high(0)
        change(1)
        add_tensor(0, 0)
        add(1, low)
        make_hidden(3)
        add_tensor_rest(0)
        add_high(1)
        change(2)
        join_rest(0)
        add_tensor(1, 0)
        add(2, low)
        change(3)
        add_tensor_rest(1)
        add(3, low)
        add_high(2)
        join_rest(1)
        add_tensor(2, 0)
        add_high(3)
        add_tensor_rest(2)
        add_tensor(3, 0)
        join_rest(2)
        add_tensor_rest(3)
        join_rest(3)

    slot_errs, hiddens = [], []
    for c in range(n_chunk):
        err = jnp.concatenate(spread[c], axis=0)
        put = tables[c] == jnp.arange(2 * sizes[c] * cap, dtype=jnp.int32)[None, :]
        picked = lax.dot_general(
            put.astype(BF16), err, (((0,), (0,)), ((), ())), preferred_element_type=F32)
        weight = jnp.concatenate([scale[k][groups_of(c)].reshape(-1, 1) for k in range(2)], axis=0)
        slot_errs.append((weight * picked).astype(BF16))
        hiddens += [near_hidden[c], far_hidden[c]]
    grad = lax.dot_general(
        jnp.concatenate(slot_errs, axis=0), jnp.concatenate(hiddens, axis=0),
        (((0,), (0,)), ((), ())), preferred_element_type=F32)
    return grad.astype(BF16)[None]


def solution(mesh):
    in_specs = (
        P(("expert", "dp"), None),
        P(("expert", "dp"), None),
        P(),
        P(),
        P(),
        P("expert", "dp", "tensor"),
        P("expert", "dp", "tensor"),
        P("expert", "dp", "tensor"),
        P("expert", "dp", "tensor"),
    )
    out_specs = P("expert", "dp", "tensor")
    return jax.shard_map(local, mesh=mesh, in_specs=in_specs, out_specs=out_specs, check_vma=False)
```

```python
import jax
import jax.numpy as jnp
from jax import lax
from jax.experimental import pallas as pl
from jax.experimental.pallas import tpu as pltpu
from jax.sharding import PartitionSpec as P

TOP = 2
BF16 = jnp.bfloat16
F32 = jnp.float32

forget_coef = 0.0625
retain_coef = 0.125


def xor_permute(block, axis, mask):
    size = lax.axis_size(axis)
    return lax.ppermute(block, axis, [(i, i ^ mask) for i in range(size)])


def bits_of(size):
    return [1 << b for b in range(size.bit_length() - 1)]


def reversed_order(size):
    order = [0]
    for bit in bits_of(size)[::-1]:
        order = order + [j | bit for j in order]
    return order


def gather_blocks(block, axis, hold=None):
    size = lax.axis_size(axis)
    blocks = {0: block}
    for bit in bits_of(size)[::-1]:
        if bit == 1 and hold:
            blocks = hold(blocks)
        for j in list(blocks):
            blocks[j ^ bit] = xor_permute(blocks[j], axis, bit)
    return [blocks[j] for j in range(size)]


class Order:
    def __init__(self):
        self.last = None

    def after(self, value, *others):
        others = others + (() if self.last is None else (self.last,))
        return lax.optimization_barrier((value, others))[0] if others else value

    def done(self, value):
        self.last = value
        return value


LITTLE = pl.CostEstimate(flops=0, bytes_accessed=0, transcendentals=0)


def params(mib):
    return pltpu.CompilerParams(vmem_limit_bytes=mib * 1024 * 1024)


def vmem():
    return pl.BlockSpec(memory_space=pltpu.VMEM)


def project_kernel(other_dp, own_first, cap, bounds, routes_ref, *refs):
    n_blocks = len(refs) - 8 - len(bounds)
    blocks, weights = refs[:n_blocks], refs[n_blocks:n_blocks + 2]
    outs, (flat_ref, row_ref, held_ref, out_ref, in_sems, out_sems) = refs[n_blocks + 2:-6], refs[-6:]
    size = routes_ref.shape[1] // (lax.axis_size("expert") * lax.axis_size("dp"))
    ff = held_ref.shape[2]
    tile = min(ff, 512)
    cuts = [(at, slice(left, left + tile)) for left in range(0, ff, tile) for at in range(2)]
    arrive = [pltpu.make_async_copy(weights[at].at[:, cols], held_ref.at[at, :, cols], in_sems.at[k])
              for k, (at, cols) in enumerate(cuts)]
    for copy in arrive:
        copy.start()
    me, dp = lax.axis_index("expert"), lax.axis_index("dp")
    n_dp = lax.axis_size("dp")
    dp = 1 - dp if other_dp else dp
    earlier = (lax.broadcasted_iota(jnp.int32, (size, size), 0)
               < lax.broadcasted_iota(jnp.int32, (size, size), 1)).astype(F32)
    slot_iota = lax.broadcasted_iota(jnp.int32, (cap, size), 0)
    for k in range(n_blocks):
        j = k + 1 if own_first and n_blocks > 1 else k
        group = me ^ j
        chosen = routes_ref[:, pl.ds(pl.multiple_of((group * n_dp + dp) * size, 128), size)] == me
        member = jnp.max(chosen.astype(F32), axis=0, keepdims=True)
        before = jnp.dot(jnp.broadcast_to(member, (8, size)), earlier, preferred_element_type=F32)[0:1]
        slot = jnp.where(member > 0.5, before, -1.0).astype(jnp.int32)
        hit = (slot == slot_iota).astype(F32).astype(BF16)
        rows = jnp.dot(hit, blocks[k][:size], preferred_element_type=F32)
        if n_blocks == 1:
            flat_ref[...] = rows
            continue
        place = jnp.where(group < me, group, group - 1) if own_first else group
        flat_ref[pl.ds(pl.multiple_of(place * cap, 8), cap)] = rows
    row_ref[...] = flat_ref[...].astype(BF16)
    leave = []
    for k, (at, cols) in enumerate(cuts):
        arrive[k].wait()
        product = jnp.dot(row_ref[...], held_ref[at, :, cols], preferred_element_type=F32)
        out_ref[at, :, cols] = product.astype(out_ref.dtype)
        for c, (first, last) in enumerate(bounds):
            leave.append(pltpu.make_async_copy(
                out_ref.at[at, first:last, cols], outs[c].at[at, :, cols], out_sems.at[k, c]))
            leave[-1].start()
    for copy in leave:
        copy.wait()


def project(other_dp, own_first, cap, routes, blocks, w_gate, w_up, bounds, dtype):
    depth, ff = w_gate.shape
    n_blocks = len(blocks)
    n_cuts = 2 * (ff // min(ff, 512))
    return pl.pallas_call(
        lambda *refs: project_kernel(other_dp, own_first, cap, bounds, *refs),
        in_specs=[vmem()] * (n_blocks + 1) + [pl.BlockSpec(memory_space=pl.ANY)] * 2,
        out_specs=[pl.BlockSpec(memory_space=pltpu.HBM)] * len(bounds),
        out_shape=[jax.ShapeDtypeStruct((2, b - a, ff), dtype) for a, b in bounds],
        scratch_shapes=[
            pltpu.VMEM((bounds[-1][1], depth), F32),
            pltpu.VMEM((bounds[-1][1], depth), BF16),
            pltpu.VMEM((2, depth, ff), BF16),
            pltpu.VMEM((2, bounds[-1][1], ff), dtype),
            pltpu.SemaphoreType.DMA((n_cuts,)),
            pltpu.SemaphoreType.DMA((n_cuts, len(bounds))),
        ],
        compiler_params=params(52),
        cost_estimate=LITTLE,
    )(routes, *blocks, w_gate, w_up)


def hide_kernel(chunk, places, kept_ref, *refs):
    came_refs, out_ref = refs[:-1], refs[-1]

    def write(came_ref):
        gate = kept_ref[0] + came_ref[0].astype(F32)
        up = kept_ref[1] + came_ref[1].astype(F32)
        out_ref[...] = (gate / (1.0 + jnp.exp(-gate)) * up).astype(BF16)

    if len(places) == 1:
        write(came_refs[0])
        return
    me = lax.axis_index("expert")
    at = jnp.where(me == chunk, 0, jnp.where(chunk < me, chunk + 1, chunk))
    for place, came_ref in zip(places, came_refs):
        @pl.when(at == place)
        def _(came_ref=came_ref):
            write(came_ref)


def hide(chunk, kept, came):
    _, rows, ff = kept.shape
    places = sorted(came)
    return pl.pallas_call(
        lambda *refs: hide_kernel(chunk, places, *refs),
        in_specs=[vmem()] * (1 + len(places)),
        out_specs=vmem(),
        out_shape=jax.ShapeDtypeStruct((rows, ff), BF16),
        compiler_params=params(12),
        cost_estimate=LITTLE,
    )(kept, *[came[p] for p in places])


def down_kernel(chunk, near_ref, far_ref, trained_ref, frozen_ref, coef_ref, table_ref, keep_ref, send_ref, hid_ref):
    slots = near_ref.shape[0]
    hid_ref[:slots] = near_ref[...]
    hid_ref[slots:] = far_ref[...]
    contract = (((1,), (1,)), ((), ()))
    slot = lax.broadcasted_iota(jnp.int32, (table_ref.shape[1], 2 * slots), 1)
    put = (table_ref[chunk] == slot).astype(F32).astype(BF16)
    half = put.shape[0] // 2
    width = trained_ref.shape[0]
    tile = 256
    for left in range(0, width, tile):
        cols = slice(left, left + tile)
        hidden = hid_ref[...]
        trained = lax.dot_general(hidden, trained_ref[cols], contract, preferred_element_type=F32)
        frozen = lax.dot_general(hidden, frozen_ref[cols], contract, preferred_element_type=F32)
        change = coef_ref[chunk, :, 0:1] * trained - coef_ref[chunk, :, 1:2] * frozen
        high = change.astype(BF16)
        low = (change - high.astype(F32)).astype(BF16)
        part = (jnp.dot(put, high, preferred_element_type=F32)
                + jnp.dot(put, low, preferred_element_type=F32))
        keep_ref[:, cols] = part[:half]
        send_ref[:, cols] = part[half:].astype(BF16)


def down(chunk, near, far, trained, frozen, coef, table):
    slots, ff = near.shape
    width = trained.shape[0]
    rows = table.shape[1]
    return pl.pallas_call(
        lambda *refs: down_kernel(chunk, *refs),
        in_specs=[vmem()] * 6,
        out_specs=[vmem()] * 2,
        out_shape=[
            jax.ShapeDtypeStruct((rows // 2, width), F32),
            jax.ShapeDtypeStruct((rows // 2, width), BF16),
        ],
        scratch_shapes=[pltpu.VMEM((2 * slots, ff), BF16)],
        compiler_params=params(12),
        cost_estimate=LITTLE,
    )(near, far, trained, frozen, coef, table)


def slot_table(group_routes, expert, capacity):
    member = jnp.any(group_routes == expert, axis=2).astype(jnp.int32)
    position = jnp.cumsum(member, axis=1) - member
    return jnp.where(member > 0, position, -1)


def local(
    tokens, chosen_logits, routes, forget_flag, steer, w_gate, w_up, down_frozen, down_trained
):
    n_exp = lax.axis_size("expert")
    n_ten = lax.axis_size("tensor")
    n_dp = lax.axis_size("dp")
    n_tok = tokens.shape[0]
    width = w_gate.shape[1]
    cap = min(n_tok, n_tok * TOP // n_exp + n_tok * TOP // (4 * n_exp))
    me = lax.axis_index("expert")
    my_dp = lax.axis_index("dp")
    w_gate, w_up, down_frozen, down_trained = w_gate[0], w_up[0], down_frozen[0], down_trained[0]
    if n_exp == 4 and n_tok * n_dp // n_ten >= 64:
        sizes = [1] * n_exp
    else:
        sizes = [n_exp]
    n_chunk = len(sizes)
    starts = [sum(sizes[:c]) for c in range(n_chunk)]

    order = Order()
    relative = me ^ jnp.arange(n_exp, dtype=jnp.int32)
    exp_order = jnp.asarray(reversed_order(n_exp), jnp.int32)
    shares = [size * n_tok // n_exp for size in sizes]

    first_w = 1.0 / (1.0 + jnp.exp(chosen_logits[:, 1] - chosen_logits[:, 0]))
    rest_w, parts = first_w, []
    for _ in range(3):
        parts.append(rest_w.astype(BF16))
        rest_w = rest_w - parts[-1].astype(F32)
    below = jnp.pad(jnp.stack(parts, axis=0), ((0, 13), (0, width - n_tok)))
    mine = lax.dynamic_slice_in_dim(tokens, my_dp * width, width, 1)
    other = lax.dynamic_slice_in_dim(tokens, (1 - my_dp) * width, width, 1)
    mine_below = jnp.concatenate([mine, below], axis=0)
    other_came = xor_permute(jnp.concatenate([other, below], axis=0), "dp", 1)
    routes_t = routes.T

    def both_sides(a):
        return jnp.stack([lax.dynamic_index_in_dim(a, dp, 1, keepdims=False) for dp in (my_dp, 1 - my_dp)], axis=0)

    slot_iota = jnp.arange(cap, dtype=jnp.int32)

    def swap(value):
        return xor_permute(value, "dp", 1)

    def groups_of(c):
        return slice(starts[c], starts[c] + sizes[c])

    bounds = [(starts[c] * cap, (starts[c] + sizes[c]) * cap) for c in range(n_chunk)]
    if n_chunk > 1:
        own = []

        def own_first(blocks):
            own.extend(order.done(project(
                False, True, cap, routes_t, [mine_below], w_gate, w_up, bounds[:1], BF16)))
            return order.after(blocks)

        near = gather_blocks(mine_below, "expert", own_first)
        other_came = order.after(other_came)
        rest = project(False, True, cap, routes_t, order.after(near[1:]), w_gate, w_up, bounds[:-1], BF16)
        sent = own + list(order.done(rest))
    else:
        near = gather_blocks(mine_below, "expert")
        sent = order.done(project(False, False, cap, routes_t, near, w_gate, w_up, bounds, BF16))
    far = gather_blocks(other_came, "expert", order.after)
    ahead = min(3, n_chunk)
    came = [swap(v) for v in sent[:ahead]] + [None] * (n_chunk - ahead)
    kept = order.done(project(True, False, cap, routes_t, order.after(far), w_gate, w_up, bounds, F32))

    def make_tables():
        size, share = sizes[0], shares[0]
        late_routes, late_flags, late_near, late_far, late_steer = order.after(
            (routes, forget_flag, near, far, steer))
        late_routes = both_sides(late_routes.reshape(n_exp, n_dp, n_tok, TOP))
        flags = both_sides(late_flags.reshape(n_exp, n_dp, n_tok).astype(F32))
        late_slots = jnp.stack([slot_table(r, me, cap) for r in late_routes], axis=0)
        stacks = [jnp.stack(late_near, axis=0), jnp.stack(late_far, axis=0)]
        all_w = jnp.stack([jnp.sum(b[:, n_tok:n_tok + 3, :n_tok].astype(F32), axis=1) for b in stacks], axis=0)
        all_w = jnp.take(all_w, relative, axis=1)
        weight = jnp.where(late_routes[:, :, :, 0] == me, all_w, 1.0 - all_w)
        in_slot = slot_iota[None, None, :, None] == late_slots[:, :, None, :]
        spread_w = jnp.where(in_slot, weight[:, :, None, :], 0.0)
        coefs = jnp.stack(
            [jnp.sum(spread_w, axis=3), jnp.sum(spread_w * (1.0 - flags)[:, :, None, :], axis=3)], axis=3)
        coefs = coefs.reshape(2, n_chunk, size * cap, 2).swapaxes(0, 1).reshape(n_chunk, 2 * size * cap, 2)
        base = (jnp.arange(2, dtype=jnp.int32)[:, None, None] * (size * cap)
                + (jnp.arange(n_exp, dtype=jnp.int32) % size)[None, :, None] * cap)
        table = jnp.where(late_slots < 0, -1, late_slots + base).reshape(2, n_chunk, n_exp, share)
        table = jnp.take(table.transpose(1, 2, 0, 3), exp_order ^ me, axis=1).reshape(n_chunk, -1, 1)
        my_steer = lax.dynamic_slice_in_dim(late_steer, my_dp * width, width, 0)
        first = me * share
        at = first % n_tok
        biases, factors = [], []
        for c in range(n_chunk):
            group = starts[c] + first // n_tok
            own_tok = jnp.concatenate([
                lax.dynamic_slice(b, (me ^ group, at, 0), (1, share, width))[0] for b in stacks], axis=0)
            flag = lax.dynamic_slice(flags, (0, group, at), (2, 1, share)).reshape(-1, 1)
            biases.append(flag * (own_tok.astype(F32) - my_steer[None, :]))
            factors.append(retain_coef - (retain_coef - forget_coef) * flag)
        return order.done(lax.optimization_barrier((coefs, table, biases, factors)))

    far_hidden, near_hidden = [None] * n_chunk, [None] * n_chunk

    def make_hidden(c):
        places = {0, c, min(c + 1, n_chunk - 1)} - ({c} if c == 0 and n_chunk > 1 else set()) | {0}
        far_hidden[c] = order.done(hide(c, order.after(kept[c]), {p: came[p] for p in places}))
        near_hidden[c] = swap(far_hidden[c])

    def send_sums(c):
        came[c] = swap(order.after(sent[c]))

    exp_bits, ten_bits = bits_of(n_exp), bits_of(n_ten)[::-1]
    sums = [None] * n_chunk
    to_send = [None] * n_chunk
    spread = [None] * n_chunk

    def change(c):
        keep, send = order.done(down(
            c, order.after(near_hidden[c]), far_hidden[c], down_trained, down_frozen, coefs, tables))
        sums[c] = (keep, xor_permute(send, "expert", 1))

    def add(c, bit):
        keep, got = sums[c]
        total = order.after(keep) + got.astype(F32)
        if 2 * bit < n_exp:
            half = total.shape[0] // 2
            keep, send = order.done((total[:half], total[half:].astype(BF16)))
            sums[c] = (keep, xor_permute(send, "expert", 2 * bit))
            return
        spread_over(c, order.done(total), 0)

    def spread_over(c, total, step):
        bit = ten_bits[step] if c % 2 == 0 else ten_bits[-1 - step]
        sums[c] = (total, xor_permute(total.astype(BF16), "tensor", bit))

    def add_tensor(c, step):
        keep, got = sums[c]
        total = order.after(keep) + got.astype(F32)
        if step + 1 < len(ten_bits):
            spread_over(c, order.done(total), step + 1)
            return
        spread[c] = order.done(((total + biases[c]) * factors[c]).astype(BF16))
        widen(c, exp_bits[-1])

    def widen(c, bit):
        got = xor_permute(spread[c], "expert", bit)
        spread[c] = [spread[c], got]

    def join(c, bit):
        err = order.done(jnp.concatenate(order.after(spread[c]), axis=0))
        spread[c] = err
        if bit:
            widen(c, bit)


    def grad_of(chunks):
        slot_errs, hiddens = [], []
        for c in chunks:
            err = jnp.concatenate(spread[c], axis=0)
            put = tables[c] == jnp.arange(2 * sizes[c] * cap, dtype=jnp.int32)[None, :]
            picked = lax.dot_general(
                put.astype(BF16), err, (((0,), (0,)), ((), ())), preferred_element_type=F32)
            slot_errs.append((coefs[c][:, 0:1] * picked).astype(BF16))
            hiddens += [near_hidden[c], far_hidden[c]]
        return lax.dot_general(
            jnp.concatenate(slot_errs, axis=0), jnp.concatenate(hiddens, axis=0),
            (((0,), (0,)), ((), ())), preferred_element_type=F32)

    def add_high(c):
        for bit in exp_bits[1:]:
            add(c, bit)

    def add_tensor_rest(c):
        for step in range(1, len(ten_bits)):
            add_tensor(c, step)

    def join_rest(c):
        for bit in exp_bits[::-1][1:]:
            join(c, bit)

    low = exp_bits[0]
    coefs, tables, biases, factors = make_tables()
    make_hidden(0)
    if n_chunk == 1:
        change(0)
        add(0, low)
        add_high(0)
        add_tensor(0, 0)
        add_tensor_rest(0)
        join_rest(0)
    else:
        send_sums(3)
        make_hidden(1)
        change(0)
        add(0, low)
        make_hidden(2)
        add_high(0)
        change(1)
        add_tensor(0, 0)
        add(1, low)
        make_hidden(3)
        add_tensor_rest(0)
        add_high(1)
        change(2)
        join_rest(0)
        add_tensor(1, 0)
        add(2, low)
        change(3)
        add_high(2)
        add(3, low)
        add_tensor_rest(1)
        add_high(3)
        add_tensor(2, 0)
        join_rest(1)
        add_tensor(3, 0)
        add_tensor_rest(2)
        add_tensor_rest(3)
        join_rest(2)
        join_rest(3)

    return grad_of(range(n_chunk)).astype(BF16)[None]


def solution(mesh):
    in_specs = (
        P(("expert", "dp"), None),
        P(("expert", "dp"), None),
        P(),
        P(),
        P(),
        P("expert", "dp", "tensor"),
        P("expert", "dp", "tensor"),
        P("expert", "dp", "tensor"),
        P("expert", "dp", "tensor"),
    )
    out_specs = P("expert", "dp", "tensor")
    return jax.shard_map(local, mesh=mesh, in_specs=in_specs, out_specs=out_specs, check_vma=False)
```

```python
import jax
import jax.numpy as jnp
from jax import lax
from jax.experimental import pallas as pl
from jax.experimental.pallas import tpu as pltpu
from jax.sharding import PartitionSpec as P

TOP = 2
BF16 = jnp.bfloat16
F32 = jnp.float32

forget_coef = 0.0625
retain_coef = 0.125


def xor_permute(block, axis, mask):
    size = lax.axis_size(axis)
    return lax.ppermute(block, axis, [(i, i ^ mask) for i in range(size)])


def bits_of(size):
    return [1 << b for b in range(size.bit_length() - 1)]


def reversed_order(size):
    order = [0]
    for bit in bits_of(size)[::-1]:
        order = order + [j | bit for j in order]
    return order


def gather_blocks(block, axis, hold=None):
    size = lax.axis_size(axis)
    blocks = {0: block}
    for bit in bits_of(size)[::-1]:
        if bit == 1 and hold:
            blocks = hold(blocks)
        for j in list(blocks):
            blocks[j ^ bit] = xor_permute(blocks[j], axis, bit)
    return [blocks[j] for j in range(size)]


class Order:
    def __init__(self):
        self.last = None

    def after(self, value, *others):
        others = others + (() if self.last is None else (self.last,))
        return lax.optimization_barrier((value, others))[0] if others else value

    def done(self, value):
        self.last = value
        return value


LITTLE = pl.CostEstimate(flops=0, bytes_accessed=0, transcendentals=0)


def params(mib):
    return pltpu.CompilerParams(vmem_limit_bytes=mib * 1024 * 1024)


def vmem():
    return pl.BlockSpec(memory_space=pltpu.VMEM)


def project_kernel(other_dp, own_first, cap, bounds, routes_ref, *refs):
    n_blocks = len(refs) - 8 - len(bounds)
    blocks, weights = refs[:n_blocks], refs[n_blocks:n_blocks + 2]
    outs, (flat_ref, row_ref, held_ref, out_ref, in_sems, out_sems) = refs[n_blocks + 2:-6], refs[-6:]
    size = routes_ref.shape[1] // (lax.axis_size("expert") * lax.axis_size("dp"))
    ff = held_ref.shape[2]
    tile = min(ff, 512)
    cuts = [(at, slice(left, left + tile)) for left in range(0, ff, tile) for at in range(2)]
    arrive = [pltpu.make_async_copy(weights[at].at[:, cols], held_ref.at[at, :, cols], in_sems.at[k])
              for k, (at, cols) in enumerate(cuts)]
    for copy in arrive:
        copy.start()
    me, dp = lax.axis_index("expert"), lax.axis_index("dp")
    n_dp = lax.axis_size("dp")
    dp = 1 - dp if other_dp else dp
    earlier = (lax.broadcasted_iota(jnp.int32, (size, size), 0)
               < lax.broadcasted_iota(jnp.int32, (size, size), 1)).astype(F32)
    slot_iota = lax.broadcasted_iota(jnp.int32, (cap, size), 0)
    for k in range(n_blocks):
        j = k + 1 if own_first and n_blocks > 1 else k
        group = me ^ j
        chosen = routes_ref[:, pl.ds(pl.multiple_of((group * n_dp + dp) * size, 128), size)] == me
        member = jnp.max(chosen.astype(F32), axis=0, keepdims=True)
        before = jnp.dot(jnp.broadcast_to(member, (8, size)), earlier, preferred_element_type=F32)[0:1]
        slot = jnp.where(member > 0.5, before, -1.0).astype(jnp.int32)
        hit = (slot == slot_iota).astype(F32).astype(BF16)
        rows = jnp.dot(hit, blocks[k][:size], preferred_element_type=F32)
        if n_blocks == 1:
            flat_ref[...] = rows
            continue
        place = jnp.where(group < me, group, group - 1) if own_first else group
        flat_ref[pl.ds(pl.multiple_of(place * cap, 8), cap)] = rows
    row_ref[...] = flat_ref[...].astype(BF16)
    leave = []
    for k, (at, cols) in enumerate(cuts):
        arrive[k].wait()
        product = jnp.dot(row_ref[...], held_ref[at, :, cols], preferred_element_type=F32)
        out_ref[at, :, cols] = product.astype(out_ref.dtype)
        for c, (first, last) in enumerate(bounds):
            leave.append(pltpu.make_async_copy(
                out_ref.at[at, first:last, cols], outs[c].at[at, :, cols], out_sems.at[k, c]))
            leave[-1].start()
    for copy in leave:
        copy.wait()


def project(other_dp, own_first, cap, routes, blocks, w_gate, w_up, bounds, dtype):
    depth, ff = w_gate.shape
    n_blocks = len(blocks)
    n_cuts = 2 * (ff // min(ff, 512))
    return pl.pallas_call(
        lambda *refs: project_kernel(other_dp, own_first, cap, bounds, *refs),
        in_specs=[vmem()] * (n_blocks + 1) + [pl.BlockSpec(memory_space=pl.ANY)] * 2,
        out_specs=[pl.BlockSpec(memory_space=pltpu.HBM)] * len(bounds),
        out_shape=[jax.ShapeDtypeStruct((2, b - a, ff), dtype) for a, b in bounds],
        scratch_shapes=[
            pltpu.VMEM((bounds[-1][1], depth), F32),
            pltpu.VMEM((bounds[-1][1], depth), BF16),
            pltpu.VMEM((2, depth, ff), BF16),
            pltpu.VMEM((2, bounds[-1][1], ff), dtype),
            pltpu.SemaphoreType.DMA((n_cuts,)),
            pltpu.SemaphoreType.DMA((n_cuts, len(bounds))),
        ],
        compiler_params=params(52),
        cost_estimate=LITTLE,
    )(routes, *blocks, w_gate, w_up)


def hide_kernel(chunk, places, kept_ref, *refs):
    came_refs, out_ref = refs[:-1], refs[-1]

    ff = out_ref.shape[1]
    tile = min(ff, 256)

    def write(came_ref):
        @pl.loop(0, ff // tile)
        def _(k):
            cols = pl.ds(pl.multiple_of(k * tile, 128), tile)
            gate = kept_ref[0, :, cols] + came_ref[0, :, cols].astype(F32)
            up = kept_ref[1, :, cols] + came_ref[1, :, cols].astype(F32)
            out_ref[:, cols] = (gate / (1.0 + jnp.exp(-gate)) * up).astype(BF16)

    if len(places) == 1:
        write(came_refs[0])
        return
    me = lax.axis_index("expert")
    at = jnp.where(me == chunk, 0, jnp.where(chunk < me, chunk + 1, chunk))
    for place, came_ref in zip(places, came_refs):
        @pl.when(at == place)
        def _(came_ref=came_ref):
            write(came_ref)


def hide(chunk, kept, came):
    _, rows, ff = kept.shape
    places = sorted(came)
    return pl.pallas_call(
        lambda *refs: hide_kernel(chunk, places, *refs),
        in_specs=[vmem()] * (1 + len(places)),
        out_specs=vmem(),
        out_shape=jax.ShapeDtypeStruct((rows, ff), BF16),
        compiler_params=params(12),
        cost_estimate=LITTLE,
    )(kept, *[came[p] for p in places])


def down_kernel(chunk, near_ref, far_ref, trained_ref, frozen_ref, coef_ref, table_ref, keep_ref, send_ref, hid_ref):
    slots = near_ref.shape[0]
    hid_ref[:slots] = near_ref[...]
    hid_ref[slots:] = far_ref[...]
    contract = (((1,), (1,)), ((), ()))
    slot = lax.broadcasted_iota(jnp.int32, (table_ref.shape[1], 2 * slots), 1)
    put = (table_ref[chunk] == slot).astype(F32).astype(BF16)
    half = put.shape[0] // 2
    width = trained_ref.shape[0]
    tile = 256
    for left in range(0, width, tile):
        cols = slice(left, left + tile)
        hidden = hid_ref[...]
        trained = lax.dot_general(hidden, trained_ref[cols], contract, preferred_element_type=F32)
        frozen = lax.dot_general(hidden, frozen_ref[cols], contract, preferred_element_type=F32)
        change = coef_ref[chunk, :, 0:1] * trained - coef_ref[chunk, :, 1:2] * frozen
        high = change.astype(BF16)
        low = (change - high.astype(F32)).astype(BF16)
        part = (jnp.dot(put, high, preferred_element_type=F32)
                + jnp.dot(put, low, preferred_element_type=F32))
        keep_ref[:, cols] = part[:half]
        send_ref[:, cols] = part[half:].astype(BF16)


def down(chunk, near, far, trained, frozen, coef, table):
    slots, ff = near.shape
    width = trained.shape[0]
    rows = table.shape[1]
    return pl.pallas_call(
        lambda *refs: down_kernel(chunk, *refs),
        in_specs=[vmem()] * 6,
        out_specs=[vmem()] * 2,
        out_shape=[
            jax.ShapeDtypeStruct((rows // 2, width), F32),
            jax.ShapeDtypeStruct((rows // 2, width), BF16),
        ],
        scratch_shapes=[pltpu.VMEM((2 * slots, ff), BF16)],
        compiler_params=params(12),
        cost_estimate=LITTLE,
    )(near, far, trained, frozen, coef, table)


def slot_table(group_routes, expert, capacity):
    member = jnp.any(group_routes == expert, axis=2).astype(jnp.int32)
    position = jnp.cumsum(member, axis=1) - member
    return jnp.where(member > 0, position, -1)


def local(
    tokens, chosen_logits, routes, forget_flag, steer, w_gate, w_up, down_frozen, down_trained
):
    n_exp = lax.axis_size("expert")
    n_ten = lax.axis_size("tensor")
    n_dp = lax.axis_size("dp")
    n_tok = tokens.shape[0]
    width = w_gate.shape[1]
    cap = min(n_tok, n_tok * TOP // n_exp + n_tok * TOP // (4 * n_exp))
    me = lax.axis_index("expert")
    my_dp = lax.axis_index("dp")
    w_gate, w_up, down_frozen, down_trained = w_gate[0], w_up[0], down_frozen[0], down_trained[0]
    if n_exp == 4 and n_tok * n_dp // n_ten >= 64:
        sizes = [1] * n_exp
    else:
        sizes = [n_exp]
    n_chunk = len(sizes)
    starts = [sum(sizes[:c]) for c in range(n_chunk)]

    order = Order()
    relative = me ^ jnp.arange(n_exp, dtype=jnp.int32)
    exp_order = jnp.asarray(reversed_order(n_exp), jnp.int32)
    shares = [size * n_tok // n_exp for size in sizes]

    first_w = 1.0 / (1.0 + jnp.exp(chosen_logits[:, 1] - chosen_logits[:, 0]))
    rest_w, parts = first_w, []
    for _ in range(3):
        rounded = lax.reduce_precision(rest_w, 8, 7)
        parts.append(rounded.astype(BF16))
        rest_w = rest_w - rounded
    below = jnp.pad(jnp.stack(parts, axis=0), ((0, 13), (0, width - n_tok)))
    mine = lax.dynamic_slice_in_dim(tokens, my_dp * width, width, 1)
    other = lax.dynamic_slice_in_dim(tokens, (1 - my_dp) * width, width, 1)
    mine_below = jnp.concatenate([mine, below], axis=0)
    other_came = xor_permute(jnp.concatenate([other, below], axis=0), "dp", 1)
    routes_t = routes.T

    def both_sides(a):
        return jnp.stack([lax.dynamic_index_in_dim(a, dp, 1, keepdims=False) for dp in (my_dp, 1 - my_dp)], axis=0)

    slot_iota = jnp.arange(cap, dtype=jnp.int32)

    def swap(value):
        return xor_permute(value, "dp", 1)

    def groups_of(c):
        return slice(starts[c], starts[c] + sizes[c])

    bounds = [(starts[c] * cap, (starts[c] + sizes[c]) * cap) for c in range(n_chunk)]
    if n_chunk > 1:
        own = []

        def own_first(blocks):
            own.extend(order.done(project(
                False, True, cap, routes_t, [mine_below], w_gate, w_up, bounds[:1], BF16)))
            return order.after(blocks)

        near = gather_blocks(mine_below, "expert", own_first)
        other_came = order.after(other_came)
        rest = project(False, True, cap, routes_t, order.after(near[1:]), w_gate, w_up, bounds[:-1], BF16)
        sent = own + list(order.done(rest))
    else:
        near = gather_blocks(mine_below, "expert")
        sent = order.done(project(False, False, cap, routes_t, near, w_gate, w_up, bounds, BF16))
    far = gather_blocks(other_came, "expert", order.after)
    ahead = min(3, n_chunk)
    came = [swap(v) for v in sent[:ahead]] + [None] * (n_chunk - ahead)
    kept = order.done(project(True, False, cap, routes_t, order.after(far), w_gate, w_up, bounds, F32))

    def make_tables():
        size, share = sizes[0], shares[0]
        late_routes, late_flags, late_near, late_far, late_steer = order.after(
            (routes, forget_flag, near, far, steer))
        late_routes = both_sides(late_routes.reshape(n_exp, n_dp, n_tok, TOP))
        flags = both_sides(late_flags.reshape(n_exp, n_dp, n_tok).astype(F32))
        late_slots = jnp.stack([slot_table(r, me, cap) for r in late_routes], axis=0)
        stacks = [jnp.stack(late_near, axis=0), jnp.stack(late_far, axis=0)]
        all_w = jnp.stack([jnp.sum(b[:, n_tok:n_tok + 3, :n_tok].astype(F32), axis=1) for b in stacks], axis=0)
        all_w = jnp.take(all_w, relative, axis=1)
        weight = jnp.where(late_routes[:, :, :, 0] == me, all_w, 1.0 - all_w)
        in_slot = slot_iota[None, None, :, None] == late_slots[:, :, None, :]
        spread_w = jnp.where(in_slot, weight[:, :, None, :], 0.0)
        coefs = jnp.stack(
            [jnp.sum(spread_w, axis=3), jnp.sum(spread_w * (1.0 - flags)[:, :, None, :], axis=3)], axis=3)
        coefs = coefs.reshape(2, n_chunk, size * cap, 2).swapaxes(0, 1).reshape(n_chunk, 2 * size * cap, 2)
        base = (jnp.arange(2, dtype=jnp.int32)[:, None, None] * (size * cap)
                + (jnp.arange(n_exp, dtype=jnp.int32) % size)[None, :, None] * cap)
        table = jnp.where(late_slots < 0, -1, late_slots + base).reshape(2, n_chunk, n_exp, share)
        table = jnp.take(table.transpose(1, 2, 0, 3), exp_order ^ me, axis=1).reshape(n_chunk, -1, 1)
        my_steer = lax.dynamic_slice_in_dim(late_steer, my_dp * width, width, 0)
        first = me * share
        at = first % n_tok
        biases, factors = [], []
        for c in range(n_chunk):
            group = starts[c] + first // n_tok
            own_tok = jnp.concatenate([
                lax.dynamic_slice(b, (me ^ group, at, 0), (1, share, width))[0] for b in stacks], axis=0)
            flag = lax.dynamic_slice(flags, (0, group, at), (2, 1, share)).reshape(-1, 1)
            biases.append(flag * (own_tok.astype(F32) - my_steer[None, :]))
            factors.append(retain_coef - (retain_coef - forget_coef) * flag)
        return order.done(lax.optimization_barrier((coefs, table, biases, factors)))

    far_hidden, near_hidden = [None] * n_chunk, [None] * n_chunk

    def make_hidden(c):
        places = {0, c, min(c + 1, n_chunk - 1)} - ({c} if c == 0 and n_chunk > 1 else set()) | {0}
        far_hidden[c] = order.done(hide(c, order.after(kept[c]), {p: came[p] for p in places}))
        near_hidden[c] = swap(far_hidden[c])

    def send_sums(c):
        came[c] = swap(order.after(sent[c]))

    exp_bits, ten_bits = bits_of(n_exp), bits_of(n_ten)[::-1]
    sums = [None] * n_chunk
    to_send = [None] * n_chunk
    spread = [None] * n_chunk

    def change(c):
        keep, send = order.done(down(
            c, order.after(near_hidden[c]), far_hidden[c], down_trained, down_frozen, coefs, tables))
        sums[c] = (keep, xor_permute(send, "expert", 1))

    def add(c, bit):
        keep, got = sums[c]
        total = order.after(keep) + got.astype(F32)
        if 2 * bit < n_exp:
            half = total.shape[0] // 2
            keep, send = order.done((total[:half], total[half:].astype(BF16)))
            sums[c] = (keep, xor_permute(send, "expert", 2 * bit))
            return
        spread_over(c, order.done(total), 0)

    def spread_over(c, total, step):
        bit = ten_bits[step] if c % 2 == 0 else ten_bits[-1 - step]
        sums[c] = (total, xor_permute(total.astype(BF16), "tensor", bit))

    def add_tensor(c, step):
        keep, got = sums[c]
        total = order.after(keep) + got.astype(F32)
        if step + 1 < len(ten_bits):
            spread_over(c, order.done(total), step + 1)
            return
        spread[c] = order.done(((total + biases[c]) * factors[c]).astype(BF16))
        widen(c, exp_bits[-1])

    def widen(c, bit):
        got = xor_permute(spread[c], "expert", bit)
        spread[c] = [spread[c], got]

    def join(c, bit):
        err = order.done(jnp.concatenate(order.after(spread[c]), axis=0))
        spread[c] = err
        if bit:
            widen(c, bit)


    def grad_of(chunks):
        slot_errs, hiddens = [], []
        for c in chunks:
            err = jnp.concatenate(spread[c], axis=0)
            put = tables[c] == jnp.arange(2 * sizes[c] * cap, dtype=jnp.int32)[None, :]
            picked = lax.dot_general(
                put.astype(BF16), err, (((0,), (0,)), ((), ())), preferred_element_type=F32)
            slot_errs.append((coefs[c][:, 0:1] * picked).astype(BF16))
            hiddens += [near_hidden[c], far_hidden[c]]
        return lax.dot_general(
            jnp.concatenate(slot_errs, axis=0), jnp.concatenate(hiddens, axis=0),
            (((0,), (0,)), ((), ())), preferred_element_type=F32)

    def add_high(c):
        for bit in exp_bits[1:]:
            add(c, bit)

    def add_tensor_rest(c):
        for step in range(1, len(ten_bits)):
            add_tensor(c, step)

    def join_rest(c):
        for bit in exp_bits[::-1][1:]:
            join(c, bit)

    low = exp_bits[0]
    coefs, tables, biases, factors = make_tables()
    make_hidden(0)
    if n_chunk == 1:
        change(0)
        add(0, low)
        add_high(0)
        add_tensor(0, 0)
        add_tensor_rest(0)
        join_rest(0)
    else:
        send_sums(3)
        make_hidden(1)
        change(0)
        add(0, low)
        make_hidden(2)
        add_high(0)
        change(1)
        add_tensor(0, 0)
        add(1, low)
        make_hidden(3)
        add_tensor_rest(0)
        add_high(1)
        change(2)
        join_rest(0)
        add_tensor(1, 0)
        add(2, low)
        change(3)
        add_high(2)
        add(3, low)
        add_tensor_rest(1)
        add_high(3)
        add_tensor(2, 0)
        join_rest(1)
        add_tensor(3, 0)
        add_tensor_rest(2)
        add_tensor_rest(3)
        join_rest(2)
        join_rest(3)

    return grad_of(range(n_chunk)).astype(BF16)[None]


def solution(mesh):
    in_specs = (
        P(("expert", "dp"), None),
        P(("expert", "dp"), None),
        P(),
        P(),
        P(),
        P("expert", "dp", "tensor"),
        P("expert", "dp", "tensor"),
        P("expert", "dp", "tensor"),
        P("expert", "dp", "tensor"),
    )
    out_specs = P("expert", "dp", "tensor")
    return jax.shard_map(local, mesh=mesh, in_specs=in_specs, out_specs=out_specs, check_vma=False)
```

```python
import jax
import jax.numpy as jnp
from jax import lax
from jax.experimental import pallas as pl
from jax.experimental.pallas import tpu as pltpu
from jax.sharding import PartitionSpec as P

TOP = 2
BF16 = jnp.bfloat16
F32 = jnp.float32

forget_coef = 0.0625
retain_coef = 0.125


def xor_permute(block, axis, mask):
    size = lax.axis_size(axis)
    return lax.ppermute(block, axis, [(i, i ^ mask) for i in range(size)])


def bits_of(size):
    return [1 << b for b in range(size.bit_length() - 1)]


def reversed_order(size):
    order = [0]
    for bit in bits_of(size)[::-1]:
        order = order + [j | bit for j in order]
    return order


def gather_blocks(block, axis, hold=None):
    size = lax.axis_size(axis)
    blocks = {0: block}
    for bit in bits_of(size)[::-1]:
        if bit == 1 and hold:
            blocks = hold(blocks)
        for j in list(blocks):
            blocks[j ^ bit] = xor_permute(blocks[j], axis, bit)
    return [blocks[j] for j in range(size)]


class Order:
    def __init__(self):
        self.last = None

    def after(self, value, *others):
        others = others + (() if self.last is None else (self.last,))
        return lax.optimization_barrier((value, others))[0] if others else value

    def done(self, value):
        self.last = value
        return value


LITTLE = pl.CostEstimate(flops=0, bytes_accessed=0, transcendentals=0)


def params(mib):
    return pltpu.CompilerParams(vmem_limit_bytes=mib * 1024 * 1024)


def vmem():
    return pl.BlockSpec(memory_space=pltpu.VMEM)


def project_kernel(other_dp, own_first, cap, bounds, routes_ref, *refs):
    n_blocks = len(refs) - 8 - len(bounds)
    blocks, weights = refs[:n_blocks], refs[n_blocks:n_blocks + 2]
    outs, (flat_ref, row_ref, held_ref, out_ref, in_sems, out_sems) = refs[n_blocks + 2:-6], refs[-6:]
    size = routes_ref.shape[1] // (lax.axis_size("expert") * lax.axis_size("dp"))
    ff = held_ref.shape[2]
    tile = min(ff, 256)
    cuts = [(at, slice(left, left + tile)) for left in range(0, ff, tile) for at in range(2)]
    arrive = [pltpu.make_async_copy(weights[at].at[:, cols], held_ref.at[at, :, cols], in_sems.at[k])
              for k, (at, cols) in enumerate(cuts)]
    for copy in arrive:
        copy.start()
    me, dp = lax.axis_index("expert"), lax.axis_index("dp")
    n_dp = lax.axis_size("dp")
    dp = 1 - dp if other_dp else dp
    earlier = (lax.broadcasted_iota(jnp.int32, (size, size), 0)
               < lax.broadcasted_iota(jnp.int32, (size, size), 1)).astype(F32)
    slot_iota = lax.broadcasted_iota(jnp.int32, (cap, size), 0)
    for k in range(n_blocks):
        j = k + 1 if own_first and n_blocks > 1 else k
        group = me ^ j
        chosen = routes_ref[:, pl.ds(pl.multiple_of((group * n_dp + dp) * size, 128), size)] == me
        member = jnp.max(chosen.astype(F32), axis=0, keepdims=True)
        before = jnp.dot(jnp.broadcast_to(member, (8, size)), earlier, preferred_element_type=F32)[0:1]
        slot = jnp.where(member > 0.5, before, -1.0).astype(jnp.int32)
        hit = (slot == slot_iota).astype(F32).astype(BF16)
        rows = jnp.dot(hit, blocks[k][:size], preferred_element_type=F32)
        if n_blocks == 1:
            flat_ref[...] = rows
            continue
        place = jnp.where(group < me, group, group - 1) if own_first else group
        flat_ref[pl.ds(pl.multiple_of(place * cap, 8), cap)] = rows
    row_ref[...] = flat_ref[...].astype(BF16)
    leave = []
    for k, (at, cols) in enumerate(cuts):
        arrive[k].wait()
        product = jnp.dot(row_ref[...], held_ref[at, :, cols], preferred_element_type=F32)
        out_ref[at, :, cols] = product.astype(out_ref.dtype)
        for c, (first, last) in enumerate(bounds):
            leave.append(pltpu.make_async_copy(
                out_ref.at[at, first:last, cols], outs[c].at[at, :, cols], out_sems.at[k, c]))
            leave[-1].start()
    for copy in leave:
        copy.wait()


def project(other_dp, own_first, cap, routes, blocks, w_gate, w_up, bounds, dtype):
    depth, ff = w_gate.shape
    n_blocks = len(blocks)
    n_cuts = 2 * (ff // min(ff, 256))
    return pl.pallas_call(
        lambda *refs: project_kernel(other_dp, own_first, cap, bounds, *refs),
        in_specs=[vmem()] * (n_blocks + 1) + [pl.BlockSpec(memory_space=pl.ANY)] * 2,
        out_specs=[pl.BlockSpec(memory_space=pltpu.HBM)] * len(bounds),
        out_shape=[jax.ShapeDtypeStruct((2, b - a, ff), dtype) for a, b in bounds],
        scratch_shapes=[
            pltpu.VMEM((bounds[-1][1], depth), F32),
            pltpu.VMEM((bounds[-1][1], depth), BF16),
            pltpu.VMEM((2, depth, ff), BF16),
            pltpu.VMEM((2, bounds[-1][1], ff), dtype),
            pltpu.SemaphoreType.DMA((n_cuts,)),
            pltpu.SemaphoreType.DMA((n_cuts, len(bounds))),
        ],
        compiler_params=params(52),
        cost_estimate=LITTLE,
    )(routes, *blocks, w_gate, w_up)


def hide_kernel(chunk, places, kept_ref, *refs):
    came_refs, out_ref = refs[:-1], refs[-1]

    ff = out_ref.shape[1]
    tile = min(ff, 256)

    def write(came_ref):
        @pl.loop(0, ff // tile)
        def _(k):
            cols = pl.ds(pl.multiple_of(k * tile, 128), tile)
            gate = kept_ref[0, :, cols] + came_ref[0, :, cols].astype(F32)
            up = kept_ref[1, :, cols] + came_ref[1, :, cols].astype(F32)
            out_ref[:, cols] = (gate / (1.0 + jnp.exp(-gate)) * up).astype(BF16)

    if len(places) == 1:
        write(came_refs[0])
        return
    me = lax.axis_index("expert")
    at = jnp.where(me == chunk, 0, jnp.where(chunk < me, chunk + 1, chunk))
    for place, came_ref in zip(places, came_refs):
        @pl.when(at == place)
        def _(came_ref=came_ref):
            write(came_ref)


def hide(chunk, kept, came):
    _, rows, ff = kept.shape
    places = sorted(came)
    return pl.pallas_call(
        lambda *refs: hide_kernel(chunk, places, *refs),
        in_specs=[vmem()] * (1 + len(places)),
        out_specs=vmem(),
        out_shape=jax.ShapeDtypeStruct((rows, ff), BF16),
        compiler_params=params(12),
        cost_estimate=LITTLE,
    )(kept, *[came[p] for p in places])


def down_kernel(chunk, near_ref, far_ref, trained_ref, frozen_ref, coef_ref, table_ref, keep_ref, send_ref, hid_ref):
    slots = near_ref.shape[0]
    hid_ref[:slots] = near_ref[...]
    hid_ref[slots:] = far_ref[...]
    contract = (((1,), (1,)), ((), ()))
    slot = lax.broadcasted_iota(jnp.int32, (table_ref.shape[1], 2 * slots), 1)
    put = (table_ref[chunk] == slot).astype(F32).astype(BF16)
    half = put.shape[0] // 2
    width = trained_ref.shape[0]
    tile = 256
    for left in range(0, width, tile):
        cols = slice(left, left + tile)
        hidden = hid_ref[...]
        trained = lax.dot_general(hidden, trained_ref[cols], contract, preferred_element_type=F32)
        frozen = lax.dot_general(hidden, frozen_ref[cols], contract, preferred_element_type=F32)
        change = coef_ref[chunk, :, 0:1] * trained - coef_ref[chunk, :, 1:2] * frozen
        high = change.astype(BF16)
        low = (change - high.astype(F32)).astype(BF16)
        part = (jnp.dot(put, high, preferred_element_type=F32)
                + jnp.dot(put, low, preferred_element_type=F32))
        keep_ref[:, cols] = part[:half]
        send_ref[:, cols] = part[half:].astype(BF16)


def down(chunk, near, far, trained, frozen, coef, table):
    slots, ff = near.shape
    width = trained.shape[0]
    rows = table.shape[1]
    return pl.pallas_call(
        lambda *refs: down_kernel(chunk, *refs),
        in_specs=[vmem()] * 6,
        out_specs=[vmem()] * 2,
        out_shape=[
            jax.ShapeDtypeStruct((rows // 2, width), F32),
            jax.ShapeDtypeStruct((rows // 2, width), BF16),
        ],
        scratch_shapes=[pltpu.VMEM((2 * slots, ff), BF16)],
        compiler_params=params(12),
        cost_estimate=LITTLE,
    )(near, far, trained, frozen, coef, table)


def slot_table(group_routes, expert, capacity):
    member = jnp.any(group_routes == expert, axis=2).astype(jnp.int32)
    position = jnp.cumsum(member, axis=1) - member
    return jnp.where(member > 0, position, -1)


def local(
    tokens, chosen_logits, routes, forget_flag, steer, w_gate, w_up, down_frozen, down_trained
):
    n_exp = lax.axis_size("expert")
    n_ten = lax.axis_size("tensor")
    n_dp = lax.axis_size("dp")
    n_tok = tokens.shape[0]
    width = w_gate.shape[1]
    cap = min(n_tok, n_tok * TOP // n_exp + n_tok * TOP // (4 * n_exp))
    me = lax.axis_index("expert")
    my_dp = lax.axis_index("dp")
    w_gate, w_up, down_frozen, down_trained = w_gate[0], w_up[0], down_frozen[0], down_trained[0]
    if n_exp == 4 and n_tok * n_dp // n_ten >= 64:
        sizes = [1] * n_exp
    else:
        sizes = [n_exp]
    n_chunk = len(sizes)
    starts = [sum(sizes[:c]) for c in range(n_chunk)]

    order = Order()
    relative = me ^ jnp.arange(n_exp, dtype=jnp.int32)
    exp_order = jnp.asarray(reversed_order(n_exp), jnp.int32)
    shares = [size * n_tok // n_exp for size in sizes]

    first_w = 1.0 / (1.0 + jnp.exp(chosen_logits[:, 1] - chosen_logits[:, 0]))
    rest_w, parts = first_w, []
    for _ in range(3):
        rounded = lax.reduce_precision(rest_w, 8, 7)
        parts.append(rounded.astype(BF16))
        rest_w = rest_w - rounded
    below = jnp.pad(jnp.stack(parts, axis=0), ((0, 13), (0, width - n_tok)))
    mine = lax.dynamic_slice_in_dim(tokens, my_dp * width, width, 1)
    other = lax.dynamic_slice_in_dim(tokens, (1 - my_dp) * width, width, 1)
    mine_below = jnp.concatenate([mine, below], axis=0)
    other_came = xor_permute(jnp.concatenate([other, below], axis=0), "dp", 1)
    routes_t = routes.T

    def both_sides(a):
        return jnp.stack([lax.dynamic_index_in_dim(a, dp, 1, keepdims=False) for dp in (my_dp, 1 - my_dp)], axis=0)

    slot_iota = jnp.arange(cap, dtype=jnp.int32)

    def swap(value):
        return xor_permute(value, "dp", 1)

    def groups_of(c):
        return slice(starts[c], starts[c] + sizes[c])

    bounds = [(starts[c] * cap, (starts[c] + sizes[c]) * cap) for c in range(n_chunk)]
    if n_chunk > 1:
        own = []

        def own_first(blocks):
            own.extend(order.done(project(
                False, True, cap, routes_t, [mine_below], w_gate, w_up, bounds[:1], BF16)))
            return order.after(blocks)

        near = gather_blocks(mine_below, "expert", own_first)
        other_came = order.after(other_came)
        rest = project(False, True, cap, routes_t, order.after(near[1:]), w_gate, w_up, bounds[:-1], BF16)
        sent = own + list(order.done(rest))
    else:
        near = gather_blocks(mine_below, "expert")
        sent = order.done(project(False, False, cap, routes_t, near, w_gate, w_up, bounds, BF16))
    far = gather_blocks(other_came, "expert", order.after)
    ahead = min(3, n_chunk)
    came = [swap(v) for v in sent[:ahead]] + [None] * (n_chunk - ahead)
    kept = order.done(project(True, False, cap, routes_t, order.after(far), w_gate, w_up, bounds, F32))

    def make_tables():
        size, share = sizes[0], shares[0]
        late_routes, late_flags, late_near, late_far, late_steer = order.after(
            (routes, forget_flag, near, far, steer))
        late_routes = both_sides(late_routes.reshape(n_exp, n_dp, n_tok, TOP))
        flags = both_sides(late_flags.reshape(n_exp, n_dp, n_tok).astype(F32))
        late_slots = jnp.stack([slot_table(r, me, cap) for r in late_routes], axis=0)
        stacks = [jnp.stack(late_near, axis=0), jnp.stack(late_far, axis=0)]
        all_w = jnp.stack([jnp.sum(b[:, n_tok:n_tok + 3, :n_tok].astype(F32), axis=1) for b in stacks], axis=0)
        all_w = jnp.take(all_w, relative, axis=1)
        weight = jnp.where(late_routes[:, :, :, 0] == me, all_w, 1.0 - all_w)
        in_slot = slot_iota[None, None, :, None] == late_slots[:, :, None, :]
        spread_w = jnp.where(in_slot, weight[:, :, None, :], 0.0)
        coefs = jnp.stack(
            [jnp.sum(spread_w, axis=3), jnp.sum(spread_w * (1.0 - flags)[:, :, None, :], axis=3)], axis=3)
        coefs = coefs.reshape(2, n_chunk, size * cap, 2).swapaxes(0, 1).reshape(n_chunk, 2 * size * cap, 2)
        base = (jnp.arange(2, dtype=jnp.int32)[:, None, None] * (size * cap)
                + (jnp.arange(n_exp, dtype=jnp.int32) % size)[None, :, None] * cap)
        table = jnp.where(late_slots < 0, -1, late_slots + base).reshape(2, n_chunk, n_exp, share)
        table = jnp.take(table.transpose(1, 2, 0, 3), exp_order ^ me, axis=1).reshape(n_chunk, -1, 1)
        my_steer = lax.dynamic_slice_in_dim(late_steer, my_dp * width, width, 0)
        first = me * share
        at = first % n_tok
        biases, factors = [], []
        for c in range(n_chunk):
            group = starts[c] + first // n_tok
            own_tok = jnp.concatenate([
                lax.dynamic_slice(b, (me ^ group, at, 0), (1, share, width))[0] for b in stacks], axis=0)
            flag = lax.dynamic_slice(flags, (0, group, at), (2, 1, share)).reshape(-1, 1)
            biases.append(flag * (own_tok.astype(F32) - my_steer[None, :]))
            factors.append(retain_coef - (retain_coef - forget_coef) * flag)
        return order.done(lax.optimization_barrier((coefs, table, biases, factors)))

    far_hidden, near_hidden = [None] * n_chunk, [None] * n_chunk

    def make_hidden(c):
        places = {0, c, min(c + 1, n_chunk - 1)} - ({c} if c == 0 and n_chunk > 1 else set()) | {0}
        far_hidden[c] = order.done(hide(c, order.after(kept[c]), {p: came[p] for p in places}))
        near_hidden[c] = swap(far_hidden[c])

    def send_sums(c):
        came[c] = swap(order.after(sent[c]))

    exp_bits, ten_bits = bits_of(n_exp), bits_of(n_ten)[::-1]
    sums = [None] * n_chunk
    to_send = [None] * n_chunk
    spread = [None] * n_chunk

    def change(c):
        keep, send = order.done(down(
            c, order.after(near_hidden[c]), far_hidden[c], down_trained, down_frozen, coefs, tables))
        sums[c] = (keep, xor_permute(send, "expert", 1))

    def add(c, bit):
        keep, got = sums[c]
        total = order.after(keep) + got.astype(F32)
        if 2 * bit < n_exp:
            half = total.shape[0] // 2
            keep, send = order.done((total[:half], total[half:].astype(BF16)))
            sums[c] = (keep, xor_permute(send, "expert", 2 * bit))
            return
        spread_over(c, order.done(total), 0)

    def spread_over(c, total, step):
        bit = ten_bits[step] if c % 2 == 0 else ten_bits[-1 - step]
        sums[c] = (total, xor_permute(total.astype(BF16), "tensor", bit))

    def add_tensor(c, step):
        keep, got = sums[c]
        total = order.after(keep) + got.astype(F32)
        if step + 1 < len(ten_bits):
            spread_over(c, order.done(total), step + 1)
            return
        spread[c] = order.done(((total + biases[c]) * factors[c]).astype(BF16))
        widen(c, exp_bits[-1])

    def widen(c, bit):
        got = xor_permute(spread[c], "expert", bit)
        spread[c] = [spread[c], got]

    def join(c, bit):
        err = order.done(jnp.concatenate(order.after(spread[c]), axis=0))
        spread[c] = err
        if bit:
            widen(c, bit)


    def grad_of(chunks):
        slot_errs, hiddens = [], []
        for c in chunks:
            err = jnp.concatenate(spread[c], axis=0)
            put = tables[c] == jnp.arange(2 * sizes[c] * cap, dtype=jnp.int32)[None, :]
            picked = lax.dot_general(
                put.astype(BF16), err, (((0,), (0,)), ((), ())), preferred_element_type=F32)
            slot_errs.append((coefs[c][:, 0:1] * picked).astype(BF16))
            hiddens += [near_hidden[c], far_hidden[c]]
        return lax.dot_general(
            jnp.concatenate(slot_errs, axis=0), jnp.concatenate(hiddens, axis=0),
            (((0,), (0,)), ((), ())), preferred_element_type=F32)

    def add_high(c):
        for bit in exp_bits[1:]:
            add(c, bit)

    def add_tensor_rest(c):
        for step in range(1, len(ten_bits)):
            add_tensor(c, step)

    def join_rest(c):
        for bit in exp_bits[::-1][1:]:
            join(c, bit)

    low = exp_bits[0]
    coefs, tables, biases, factors = make_tables()
    make_hidden(0)
    if n_chunk == 1:
        change(0)
        add(0, low)
        add_high(0)
        add_tensor(0, 0)
        add_tensor_rest(0)
        join_rest(0)
    else:
        send_sums(3)
        make_hidden(1)
        change(0)
        add(0, low)
        make_hidden(2)
        add_high(0)
        change(1)
        add_tensor(0, 0)
        add(1, low)
        make_hidden(3)
        add_tensor_rest(0)
        add_high(1)
        change(2)
        join_rest(0)
        add_tensor(1, 0)
        add(2, low)
        change(3)
        add_high(2)
        add(3, low)
        add_tensor_rest(1)
        add_high(3)
        add_tensor(2, 0)
        join_rest(1)
        add_tensor(3, 0)
        add_tensor_rest(2)
        add_tensor_rest(3)
        join_rest(2)
        join_rest(3)

    return grad_of(range(n_chunk)).astype(BF16)[None]


def solution(mesh):
    in_specs = (
        P(("expert", "dp"), None),
        P(("expert", "dp"), None),
        P(),
        P(),
        P(),
        P("expert", "dp", "tensor"),
        P("expert", "dp", "tensor"),
        P("expert", "dp", "tensor"),
        P("expert", "dp", "tensor"),
    )
    out_specs = P("expert", "dp", "tensor")
    return jax.shard_map(local, mesh=mesh, in_specs=in_specs, out_specs=out_specs, check_vma=False)
```
